32 devices in a mesh: row: 4 (over y, x), col: 8 (over z, core).
Axes of the slice: x: 2, y: 2, z: 4, core: 2. Of those that a mesh axis runs over, the one named last changes fastest.
Arguments:
- inverse_block: float32 [12288, 12288], P('row', 'col'), may hold values from -6 to 6
- factor_panel: float32 [3, 12288, 256], P(None, ('row', 'col')), may hold values from -0.0546875 to 0.0546875
- diag_inverse: float32 [3, 256, 256], P(None, 'row'), may hold values from -6 to 6
- block_lists: int32 [3, 48], replicated, may hold values from 0 to 47, as said below
- list_counts: int32 [3], replicated, may hold values from 6 to 48, as said below
Outputs:
- solved: float32 [3, 12288, 256], P(None, ('row', 'col'))
- diag_block: float32 [3, 256, 256], P(None, 'row')
The draws below stay inside these ranges and needn't reach their ends.
Inputs may be any that keep to these rules, and one draw needn't show every extreme that they name: `block_lists`: row k is an ordering of all 48 ancestor blocks; its first list_counts[k] entries are the blocks listed for supernode k. `list_counts`: one supernode lists all 48 blocks and one lists 48 // 8 of them.
All inputs are finite; a program needn't handle non-finite values.
Results may differ from the reference program's by a relative error of at most 0.000071.
Values sent between devices are 32-bit elements; how exact they have to be, the bound alone decides.
A program may use at most 64 MiB of HBM per device.

```python
import jax
import jax.numpy as jnp
from jax import lax

NA = 12288
W = 256
BLK = 256
NSN = 3
NB = 48


def listed_draw(key):
    keys = jax.random.split(jax.random.fold_in(key, 7), 5)
    orders = jnp.stack([jax.random.permutation(keys[0], NB), jax.random.permutation(keys[1], NB), jax.random.permutation(keys[2], NB)]).astype(jnp.int32)
    middle = jax.random.randint(keys[3], (), NB // 8, NB + 1).astype(jnp.int32)
    counts = jnp.stack([jnp.int32(NB), jnp.int32(NB // 8), middle])
    shuffle = jax.random.permutation(keys[4], 3)
    return (orders, counts[shuffle].astype(jnp.int32))


def draw_block_lists(key, part):
    return listed_draw(key)[0]


def draw_list_counts(key, part):
    return listed_draw(key)[1]


def spiked(values, rng, source, target, shards_of, factor):
    owner, partner = [(jnp.arange(values.shape[dim]) // (values.shape[dim] // shards_of)).reshape([-1 if axis == dim else 1 for axis in range(values.ndim)]) for dim in (source, target)]
    chosen = jax.random.permutation(rng, shards_of)[partner]
    strong = (owner == chosen) | (owner == (partner + shards_of // 2) % shards_of)
    return jnp.where(strong, factor * values, values)


def level_of(own_key, dims, cuts, least, high):
    level, own = 1.0, jax.random.fold_in(own_key, 6)
    for position, blocks in cuts:
        heights = jnp.exp(jax.random.uniform(jax.random.fold_in(own, position), (blocks,), jnp.float32, least / len(cuts), high / len(cuts)))
        level = level * jnp.repeat(heights, dims[position] // blocks).reshape([-1 if axis == position else 1 for axis in range(len(dims))])
    return level


def gaussian(rng, extent, deviation, limit, pieces=(), kind=jnp.bfloat16):
    values = jax.random.normal(rng, extent, jnp.float32) * deviation
    if len(pieces) > 0:
        values = level_of(rng, extent, pieces, -0.22, 0.18) * values
    return jnp.clip(values, min=-limit, max=limit).astype(kind)


def noise_with(rng, dims, spread, limit, cuts, heavy, kind=jnp.bfloat16):
    values = spread * jax.random.normal(rng, dims, jnp.float32)
    if cuts:
        values = values * level_of(rng, dims, cuts, -0.22, 0.18)
    return jnp.clip(spiked(values, jax.random.fold_in(rng, 3), *heavy), -limit, limit).astype(kind)


def setup_inputs(seed: int = 0) -> dict:
    streams_of = jax.random.split(jax.random.key(seed), 6)
    inverse_block = noise_with(streams_of[0], (NA, NA), 1.0, 6.0, ((0, 4), (1, 8)), (1, 0, 8, 2.0), jnp.float32)
    factor_panel = gaussian(streams_of[1], (NSN, NA, W), NA ** -0.5, 0.0546875, ((1, 32),), jnp.float32)
    diag_inverse = gaussian(streams_of[2], (NSN, W, W), 1.0, 6.0, ((1, 4),), jnp.float32)
    block_lists = draw_block_lists(jax.random.fold_in(streams_of[5], 71), 0)
    list_counts = draw_list_counts(jax.random.fold_in(streams_of[5], 71), 0)
    return {"inverse_block": inverse_block, "factor_panel": factor_panel, "diag_inverse": diag_inverse, "block_lists": block_lists, "list_counts": list_counts}


def listed_table(block_lists, list_counts, nblocks):
    entries = jnp.arange(block_lists.shape[1], dtype=jnp.int32)
    active = entries[None, :] < list_counts[:, None]
    hits = (block_lists[:, :, None] == jnp.arange(nblocks, dtype=jnp.int32)[None, None, :]) & active[:, :, None]
    return jnp.any(hits, axis=1).astype(jnp.float32)


def reference(inverse_block, factor_panel, diag_inverse, block_lists, list_counts):
    table = listed_table(block_lists, list_counts, NA // BLK)
    listed = jnp.repeat(table, BLK, axis=1)
    masked = factor_panel * listed[:, :, None]
    product = lax.map(lambda panel_rows: jnp.dot(inverse_block, panel_rows, precision=lax.Precision.HIGHEST), masked)
    solved = -listed[:, :, None] * product
    diag_block = diag_inverse - jnp.einsum("knw,knv->kwv", masked, solved, precision=lax.Precision.HIGHEST)
    return solved, diag_block
```

```python
import functools

import jax
import jax.numpy as jnp
from jax import lax
from jax.experimental import pallas as pl
from jax.experimental.pallas import tpu as pltpu
from jax.sharding import PartitionSpec as P

MESH = pl.DeviceIdType.MESH


def listed_table(block_lists, list_counts, nblocks):
    entries = jnp.arange(block_lists.shape[1], dtype=jnp.int32)
    active = entries[None, :] < list_counts[:, None]
    hits = (
        block_lists[:, :, None] == jnp.arange(nblocks, dtype=jnp.int32)[None, None, :]
    ) & active[:, :, None]
    return jnp.any(hits, axis=1).astype(jnp.float32)


def rows_mask(table, first_row, count, block):
    global_rows = first_row + jnp.arange(count, dtype=jnp.int32)
    onehot = (global_rows // block)[:, None] == jnp.arange(table.shape[1], dtype=jnp.int32)[None, :]
    return jnp.any(onehot[None] & (table > 0)[:, None, :], axis=2)


def sum_kernel(n_row, n_col, terms, out, recv, send1, recv1, send2, recv2):
    n = n_row * n_col
    row, col = lax.axis_index("row"), lax.axis_index("col")
    me = row * n_col + col

    barrier = pltpu.get_barrier_semaphore()

    def greet(d, carry):
        other = lax.rem(me + d, n)
        pl.semaphore_signal(
            barrier, inc=1, device_id=(other // n_col, lax.rem(other, n_col)), device_id_type=MESH
        )
        return carry

    lax.fori_loop(1, n, greet, 0)
    pl.semaphore_wait(barrier, n - 1)

    def spread(other):
        to_row, to_col = other // n_col, lax.rem(other, n_col)
        return pltpu.make_async_remote_copy(
            src_ref=terms.at[to_row, to_col],
            dst_ref=recv.at[me],
            send_sem=send1.at[other],
            recv_sem=recv1.at[me],
            device_id=(to_row, to_col),
            device_id_type=MESH,
        )

    def arrive(other):
        return pltpu.make_async_remote_copy(
            src_ref=terms.at[row, col],
            dst_ref=recv.at[other],
            send_sem=send1.at[other],
            recv_sem=recv1.at[other],
            device_id=(row, col),
            device_id_type=MESH,
        )

    def start1(d, carry):
        spread(lax.rem(me + d, n)).start()
        return carry

    lax.fori_loop(1, n, start1, 0)

    def add(d, total):
        other = lax.rem(me + n - d, n)
        arrive(other).wait_recv()
        return total + recv[other]

    total = lax.fori_loop(1, n, add, terms[row, col])
    out[col] = total

    def share(to_col):
        return pltpu.make_async_remote_copy(
            src_ref=out.at[col],
            dst_ref=out.at[col],
            send_sem=send2.at[to_col],
            recv_sem=recv2.at[col],
            device_id=(row, to_col),
            device_id_type=MESH,
        )

    def shared(from_col):
        return pltpu.make_async_remote_copy(
            src_ref=out.at[from_col],
            dst_ref=out.at[from_col],
            send_sem=send2.at[from_col],
            recv_sem=recv2.at[from_col],
            device_id=(row, from_col),
            device_id_type=MESH,
        )

    def start2(d, carry):
        share(lax.rem(col + d, n_col)).start()
        return carry

    lax.fori_loop(1, n_col, start2, 0)

    def end1(d, carry):
        spread(lax.rem(me + d, n)).wait_send()
        return carry

    lax.fori_loop(1, n, end1, 0)

    def end2(d, carry):
        shared(lax.rem(col + n_col - d, n_col)).wait_recv()
        share(lax.rem(col + d, n_col)).wait_send()
        return carry

    lax.fori_loop(1, n_col, end2, 0)


def sum_terms(terms, n_row, n_col):
    members, width, _ = terms.shape
    n = n_row * n_col
    lanes = 128
    depth = members * width * width // (n * lanes)
    terms = terms.reshape(members, n_row, width // n_row, width).transpose(1, 0, 2, 3)
    terms = terms.reshape(n_row, n_col, depth, lanes)
    total = pl.pallas_call(
        functools.partial(sum_kernel, n_row, n_col),
        out_shape=jax.ShapeDtypeStruct((n_col, depth, lanes), jnp.float32),
        in_specs=[pl.BlockSpec(memory_space=pltpu.VMEM)],
        out_specs=pl.BlockSpec(memory_space=pltpu.VMEM),
        scratch_shapes=[
            pltpu.VMEM((n, depth, lanes), jnp.float32),
            pltpu.SemaphoreType.DMA((n,)),
            pltpu.SemaphoreType.DMA((n,)),
            pltpu.SemaphoreType.DMA((n_col,)),
            pltpu.SemaphoreType.DMA((n_col,)),
        ],
        compiler_params=pltpu.CompilerParams(collective_id=1, has_side_effects=True),
        name="sum_terms",
    )(terms)
    return total.reshape(members, width // n_row, width)


def per_device(n_row, n_col, inverse_block, factor_panel, diag_inverse, block_lists, list_counts):
    row_id = lax.axis_index("row")
    col_id = lax.axis_index("col")
    members, local_rows, _ = factor_panel.shape
    nblocks = block_lists.shape[1]
    block = local_rows * n_row * n_col // nblocks
    n = n_row * n_col
    table = listed_table(block_lists, list_counts, nblocks)
    mask_local = rows_mask(table, (row_id * n_col + col_id) * local_rows, local_rows, block)
    masked_local = jnp.where(mask_local[:, :, None], factor_panel, 0.0)
    perm = [(p, (p % n_row) * n_col + p // n_row) for p in range(n)]
    solved = []
    for k in range(members):
        piece = lax.ppermute(masked_local[k], ("row", "col"), perm)
        columns = lax.all_gather(piece, "row", axis=0, tiled=True)
        product = jnp.dot(inverse_block, columns, precision=lax.Precision.HIGH)
        solved.append(lax.psum_scatter(product, "col", scatter_dimension=0, tiled=True))
    solved = jnp.where(mask_local[:, :, None], -jnp.stack(solved), 0.0)
    terms = jnp.einsum("knw,knv->kwv", masked_local, solved, precision=lax.Precision.HIGHEST)
    return (solved, diag_inverse - sum_terms(terms, n_row, n_col))


def solution(mesh):
    n_row, n_col = mesh.shape["row"], mesh.shape["col"]
    placed = (P("row", "col"), P(None, ("row", "col"), None), P(None, "row", None), P(), P())
    return jax.shard_map(
        functools.partial(per_device, n_row, n_col),
        mesh=mesh,
        in_specs=placed,
        out_specs=(P(None, ("row", "col"), None), P(None, "row", None)),
        check_vma=False,
    )
```

```python
import functools

import jax
import jax.numpy as jnp
from jax import lax
from jax.experimental import pallas as pl
from jax.experimental.pallas import tpu as pltpu
from jax.sharding import PartitionSpec as P

MESH = pl.DeviceIdType.MESH


def listed_table(block_lists, list_counts, nblocks):
    entries = jnp.arange(block_lists.shape[1], dtype=jnp.int32)
    active = entries[None, :] < list_counts[:, None]
    hits = (
        block_lists[:, :, None] == jnp.arange(nblocks, dtype=jnp.int32)[None, None, :]
    ) & active[:, :, None]
    return jnp.any(hits, axis=1).astype(jnp.float32)


def rows_mask(table, first_row, count, block):
    global_rows = first_row + jnp.arange(count, dtype=jnp.int32)
    onehot = (global_rows // block)[:, None] == jnp.arange(table.shape[1], dtype=jnp.int32)[None, :]
    return jnp.any(onehot[None] & (table > 0)[:, None, :], axis=2)


def sum_kernel(n_row, n_col, terms, out, recv, send1, recv1, send2, recv2):
    n = n_row * n_col
    row, col = lax.axis_index("row"), lax.axis_index("col")
    me = row * n_col + col

    barrier = pltpu.get_barrier_semaphore()

    def greet(d, carry):
        other = lax.rem(me + d, n)
        pl.semaphore_signal(
            barrier, inc=1, device_id=(other // n_col, lax.rem(other, n_col)), device_id_type=MESH
        )
        return carry

    lax.fori_loop(1, n, greet, 0)
    pl.semaphore_wait(barrier, n - 1)

    def spread(other):
        to_row, to_col = other // n_col, lax.rem(other, n_col)
        return pltpu.make_async_remote_copy(
            src_ref=terms.at[to_row, to_col],
            dst_ref=recv.at[me],
            send_sem=send1.at[other],
            recv_sem=recv1.at[me],
            device_id=(to_row, to_col),
            device_id_type=MESH,
        )

    def arrive(other):
        return pltpu.make_async_remote_copy(
            src_ref=terms.at[row, col],
            dst_ref=recv.at[other],
            send_sem=send1.at[other],
            recv_sem=recv1.at[other],
            device_id=(row, col),
            device_id_type=MESH,
        )

    def start1(d, carry):
        spread(lax.rem(me + d, n)).start()
        return carry

    lax.fori_loop(1, n, start1, 0)

    def add(d, total):
        other = lax.rem(me + n - d, n)
        arrive(other).wait_recv()
        return total + recv[other]

    total = lax.fori_loop(1, n, add, terms[row, col])
    out[col] = total

    def share(to_col):
        return pltpu.make_async_remote_copy(
            src_ref=out.at[col],
            dst_ref=out.at[col],
            send_sem=send2.at[to_col],
            recv_sem=recv2.at[col],
            device_id=(row, to_col),
            device_id_type=MESH,
        )

    def shared(from_col):
        return pltpu.make_async_remote_copy(
            src_ref=out.at[from_col],
            dst_ref=out.at[from_col],
            send_sem=send2.at[from_col],
            recv_sem=recv2.at[from_col],
            device_id=(row, from_col),
            device_id_type=MESH,
        )

    def start2(d, carry):
        share(lax.rem(col + d, n_col)).start()
        return carry

    lax.fori_loop(1, n_col, start2, 0)

    def end1(d, carry):
        spread(lax.rem(me + d, n)).wait_send()
        return carry

    lax.fori_loop(1, n, end1, 0)

    def end2(d, carry):
        shared(lax.rem(col + n_col - d, n_col)).wait_recv()
        share(lax.rem(col + d, n_col)).wait_send()
        return carry

    lax.fori_loop(1, n_col, end2, 0)


def sum_terms(terms, n_row, n_col):
    members, width, _ = terms.shape
    n = n_row * n_col
    lanes = 128
    depth = members * width * width // (n * lanes)
    terms = terms.reshape(members, n_row, width // n_row, width).transpose(1, 0, 2, 3)
    terms = terms.reshape(n_row, n_col, depth, lanes)
    total = pl.pallas_call(
        functools.partial(sum_kernel, n_row, n_col),
        out_shape=jax.ShapeDtypeStruct((n_col, depth, lanes), jnp.float32),
        in_specs=[pl.BlockSpec(memory_space=pltpu.VMEM)],
        out_specs=pl.BlockSpec(memory_space=pltpu.VMEM),
        scratch_shapes=[
            pltpu.VMEM((n, depth, lanes), jnp.float32),
            pltpu.SemaphoreType.DMA((n,)),
            pltpu.SemaphoreType.DMA((n,)),
            pltpu.SemaphoreType.DMA((n_col,)),
            pltpu.SemaphoreType.DMA((n_col,)),
        ],
        compiler_params=pltpu.CompilerParams(collective_id=1, has_side_effects=True),
        name="sum_terms",
    )(terms)
    return total.reshape(members, width // n_row, width)


def product_kernel(n_row, n_col, s_ref, x_ref, out, hop, xc, xs, hi, lo, stage, part_sum, sib, run,
                   load, s0, r0, s1, r1, s2, r2, s3, r3, s4, r4):
    n = n_row * n_col
    chips = n_col // 2
    members, local_rows, _ = x_ref.shape
    splits, part = xc.shape[2], xc.shape[3]
    group = n_row // splits
    row, col = lax.axis_index("row"), lax.axis_index("col")
    me = row * n_col + col
    chip, core = col // 2, lax.rem(col, 2)
    member_i = lax.rem(col, n_row)
    my_split = row // group
    first_i = lax.rem(row, group) * splits
    relay = lax.rem(row, group) == member_i // splits

    barrier = pltpu.get_barrier_semaphore()

    def greet(d, carry):
        other = lax.rem(me + d, n)
        pl.semaphore_signal(
            barrier, inc=1, device_id=(other // n_col, lax.rem(other, n_col)), device_id_type=MESH
        )
        return carry

    lax.fori_loop(1, n, greet, 0)
    pl.semaphore_wait(barrier, n - 1)

    def remote(src, dst, send, recv, to):
        return pltpu.make_async_remote_copy(
            src_ref=src, dst_ref=dst, send_sem=send, recv_sem=recv, device_id=to, device_id_type=MESH
        )

    def hop0(k, q):
        to_row = q * group + member_i // splits
        return to_row, remote(
            x_ref.at[k, pl.ds(q * part, part)], hop.at[k, row], s0.at[k, q], r0.at[k, row], (to_row, col)
        )

    def hop1(k, from_row):
        to_col = (from_row * n_col + col) // n_row
        return to_col, remote(
            hop.at[k, from_row],
            xc.at[k, member_i, my_split],
            s1.at[k, from_row],
            r1.at[k, lax.rem(member_i, splits)],
            (row, to_col),
        )

    def hop2(k, d):
        to_row = lax.rem(row + d, n_row)
        block = xc.at[k, pl.ds(first_i, splits), my_split]
        return remote(block, block, s2.at[k, to_row], r2.at[k, row], (to_row, col))

    for k in range(members):
        for q in range(splits):
            to_row, copy = hop0(k, q)
            pl.when(to_row != row)(copy.start)

    chunk = stage.shape[1]
    chunks = s_ref.shape[0] // chunk

    def fetch(i):
        slot = lax.rem(i, 2)
        return pltpu.make_async_copy(
            s_ref.at[pl.ds(i * chunk, chunk)], stage.at[slot], load.at[slot]
        )

    fetch(0).start()

    def split_rows(i, carry):
        @pl.when(i + 1 < chunks)
        def _():
            fetch(i + 1).start()

        fetch(i).wait()
        value = stage[lax.rem(i, 2)]
        upper = value.astype(jnp.bfloat16)
        rows = pl.ds(pl.multiple_of(i * chunk, chunk), chunk)
        hi[rows, :] = upper
        lo[rows, :] = (value - upper.astype(jnp.float32)).astype(jnp.bfloat16)
        return carry

    third = chunks // 3
    lax.fori_loop(0, third, split_rows, 0)

    for k in range(members):

        @pl.when(relay)
        def _():
            hop[k, row] = x_ref[k, pl.ds(pl.multiple_of(my_split * part, 8), part), :]
            for d in range(1, n_row):
                from_row = lax.rem(row + d, n_row)
                remote(
                    hop.at[k, from_row], hop.at[k, from_row], s0.at[k, 0], r0.at[k, from_row], (row, col)
                ).wait_recv()
            for from_row in range(n_row):
                to_col, copy = hop1(k, from_row)
                pl.when(to_col != col)(copy.start)

                @pl.when(to_col == col)
                def _():
                    xc[k, member_i, my_split] = hop[k, from_row]

    lax.fori_loop(third, 2 * third, split_rows, 0)

    for k in range(members):
        for s in range(splits):
            from_col = lax.rem(col * n_row + first_i + s, n_col)
            block = xc.at[k, first_i + s, my_split]

            @pl.when(from_col != col)
            def _():
                remote(block, block, s1.at[k, 0], r1.at[k, s], (row, col)).wait_recv()

        for d in range(1, n_row):
            hop2(k, d).start()

    lax.fori_loop(2 * third, chunks, split_rows, 0)

    def sibling(k, t):
        return remote(
            part_sum.at[k, 2 * t + 1 - core], sib.at[k, t], s3.at[k, t], r3.at[k, t],
            (row, 2 * chip + 1 - core),
        )

    width = x_ref.shape[2]

    def multiply(k):
        for d in range(1, n_row):
            from_row = lax.rem(row + d, n_row)
            block = xc.at[k, pl.ds(lax.rem(from_row, group) * splits, splits), from_row // group]
            remote(block, block, s2.at[k, 0], r2.at[k, from_row], (row, col)).wait_recv()
        for i in range(n_row):
            value = xc[k, i].reshape(local_rows, width)
            upper = value.astype(jnp.bfloat16)
            rows = pl.ds(i * local_rows, local_rows)
            xs[rows, :width] = upper
            xs[rows, width:] = (value - upper.astype(jnp.float32)).astype(jnp.bfloat16)

        def owner_rows(j, carry):
            t = lax.rem(j, chips)
            owner = 2 * t + lax.rem(core + 1 + j // chips, 2)
            rows = pl.ds(pl.multiple_of(owner * local_rows, 16), local_rows)
            both = jnp.dot(hi[rows, :], xs[...], preferred_element_type=jnp.float32)
            rest = jnp.dot(lo[rows, :], xs[:, :width], preferred_element_type=jnp.float32)
            part_sum[k, owner] = both[:, :width] + (both[:, width:] + rest)

            @pl.when(j < chips)
            def _():
                sibling(k, t).start()

            return carry

        lax.fori_loop(0, n_col, owner_rows, 0)

    def passed(k, t, slot, to_chip):
        return remote(
            part_sum.at[k, 2 * t + core], run.at[k, slot], s4.at[k, t], r4.at[k, slot],
            (row, 2 * to_chip + core),
        )

    def arrived(k, slot):
        return remote(
            run.at[k, slot], run.at[k, slot], s4.at[k, 0], r4.at[k, slot], (row, col)
        )

    def forward(k):
        for t in range(chips):
            sibling(k, t).wait()
            part_sum[k, 2 * t + core] += sib[k, t]
        for j in range(chips - 1):
            t = chips - 1 - j

            @pl.when(chip < t)
            def _():
                @pl.when(chip > 0)
                def _():
                    arrived(k, t + 1).wait_recv()
                    part_sum[k, 2 * t + core] += run[k, t + 1]

                passed(k, t, t + 1, chip + 1).start()

            @pl.when(chip > j)
            def _():
                @pl.when(chip < chips - 1)
                def _():
                    arrived(k, j).wait_recv()
                    part_sum[k, 2 * j + core] += run[k, j]

                passed(k, j, j, chip - 1).start()

    def finish(k):
        out[k] = part_sum[k, col]

        @pl.when(chip > 0)
        def _():
            arrived(k, chip + 1).wait_recv()
            out[k] += run[k, chip + 1]

        @pl.when(chip < chips - 1)
        def _():
            arrived(k, chip).wait_recv()
            out[k] += run[k, chip]

    for k in range(members):
        multiply(k)
        if k > 0:
            forward(k - 1)
    forward(members - 1)
    for k in range(members):
        finish(k)

    for k in range(members):
        for q in range(splits):
            to_row, copy = hop0(k, q)
            pl.when(to_row != row)(copy.wait_send)

        @pl.when(relay)
        def _():
            for from_row in range(n_row):
                to_col, copy = hop1(k, from_row)
                pl.when(to_col != col)(copy.wait_send)

        for d in range(1, n_row):
            hop2(k, d).wait_send()
        for t in range(chips):

            @pl.when(chip < t)
            def _():
                passed(k, t, t + 1, chip + 1).wait_send()

            @pl.when(chip > t)
            def _():
                passed(k, t, t, chip - 1).wait_send()


def product(inverse_block, masked_local, n_row, n_col):
    members, local_rows, width = masked_local.shape
    span_row, span_col = inverse_block.shape
    chips = n_col // 2
    splits = max(d for d in range(1, n_row + 1) if n_row % d == 0 and local_rows % (8 * d) == 0)
    part = local_rows // splits
    chunk = span_row // 24
    f32, bf16, sem = jnp.float32, jnp.bfloat16, pltpu.SemaphoreType.DMA
    scratch = [
        ((members, n_row, part, width), f32),
        ((members, n_row, splits, part, width), f32),
        ((span_col, 2 * width), bf16),
        ((span_row, span_col), bf16),
        ((span_row, span_col), bf16),
        ((2, chunk, span_col), f32),
        ((members, n_col, local_rows, width), f32),
        ((members, chips, local_rows, width), f32),
        ((members, chips + 1, local_rows, width), f32),
    ]
    macs = members * span_row * span_col * width
    return pl.pallas_call(
        functools.partial(product_kernel, n_row, n_col),
        out_shape=jax.ShapeDtypeStruct(masked_local.shape, f32),
        in_specs=[pl.BlockSpec(memory_space=pl.ANY), pl.BlockSpec(memory_space=pltpu.VMEM)],
        out_specs=pl.BlockSpec(memory_space=pltpu.VMEM),
        scratch_shapes=[pltpu.VMEM(shape, kind) for shape, kind in scratch]
        + [
            sem((2,)),
            sem((members, splits)), sem((members, n_row)),
            sem((members, n_row)), sem((members, splits)),
            sem((members, n_row)), sem((members, n_row)),
            sem((members, chips)), sem((members, chips)),
            sem((members, chips)), sem((members, chips + 1)),
        ],
        compiler_params=pltpu.CompilerParams(
            collective_id=2, has_side_effects=True, vmem_limit_bytes=60 * 2**20
        ),
        cost_estimate=pl.CostEstimate(
            flops=6 * macs, bytes_accessed=4 * span_row * span_col, transcendentals=0
        ),
        name="product",
    )(inverse_block, masked_local)


def per_device(n_row, n_col, inverse_block, factor_panel, diag_inverse, block_lists, list_counts):
    row_id = lax.axis_index("row")
    col_id = lax.axis_index("col")
    members, local_rows, _ = factor_panel.shape
    nblocks = block_lists.shape[1]
    block = local_rows * n_row * n_col // nblocks
    n = n_row * n_col
    table = listed_table(block_lists, list_counts, nblocks)
    mask_local = rows_mask(table, (row_id * n_col + col_id) * local_rows, local_rows, block)
    masked_local = jnp.where(mask_local[:, :, None], factor_panel, 0.0)
    solved = jnp.where(mask_local[:, :, None], -product(inverse_block, masked_local, n_row, n_col), 0.0)
    terms = jnp.einsum("knw,knv->kwv", masked_local, solved, precision=lax.Precision.HIGHEST)
    return (solved, diag_inverse - sum_terms(terms, n_row, n_col))


def solution(mesh):
    n_row, n_col = mesh.shape["row"], mesh.shape["col"]
    placed = (P("row", "col"), P(None, ("row", "col"), None), P(None, "row", None), P(), P())
    return jax.shard_map(
        functools.partial(per_device, n_row, n_col),
        mesh=mesh,
        in_specs=placed,
        out_specs=(P(None, ("row", "col"), None), P(None, "row", None)),
        check_vma=False,
    )
```

```python
import functools

import jax
import jax.numpy as jnp
from jax import lax
from jax.experimental import pallas as pl
from jax.experimental.pallas import tpu as pltpu
from jax.sharding import PartitionSpec as P

MESH = pl.DeviceIdType.MESH


def listed_table(block_lists, list_counts, nblocks):
    entries = jnp.arange(block_lists.shape[1], dtype=jnp.int32)
    active = entries[None, :] < list_counts[:, None]
    hits = (
        block_lists[:, :, None] == jnp.arange(nblocks, dtype=jnp.int32)[None, None, :]
    ) & active[:, :, None]
    return jnp.any(hits, axis=1).astype(jnp.float32)


def rows_mask(table, first_row, count, block):
    global_rows = first_row + jnp.arange(count, dtype=jnp.int32)
    onehot = (global_rows // block)[:, None] == jnp.arange(table.shape[1], dtype=jnp.int32)[None, :]
    return jnp.any(onehot[None] & (table > 0)[:, None, :], axis=2)


def sum_kernel(n_row, n_col, terms, out, recv, send1, recv1, send2, recv2):
    n = n_row * n_col
    row, col = lax.axis_index("row"), lax.axis_index("col")
    me = row * n_col + col

    barrier = pltpu.get_barrier_semaphore()

    def greet(d, carry):
        other = lax.rem(me + d, n)
        pl.semaphore_signal(
            barrier, inc=1, device_id=(other // n_col, lax.rem(other, n_col)), device_id_type=MESH
        )
        return carry

    lax.fori_loop(1, n, greet, 0)
    pl.semaphore_wait(barrier, n - 1)

    def spread(other):
        to_row, to_col = other // n_col, lax.rem(other, n_col)
        return pltpu.make_async_remote_copy(
            src_ref=terms.at[to_row, to_col],
            dst_ref=recv.at[me],
            send_sem=send1.at[other],
            recv_sem=recv1.at[me],
            device_id=(to_row, to_col),
            device_id_type=MESH,
        )

    def arrive(other):
        return pltpu.make_async_remote_copy(
            src_ref=terms.at[row, col],
            dst_ref=recv.at[other],
            send_sem=send1.at[other],
            recv_sem=recv1.at[other],
            device_id=(row, col),
            device_id_type=MESH,
        )

    def start1(d, carry):
        spread(lax.rem(me + d, n)).start()
        return carry

    lax.fori_loop(1, n, start1, 0)

    def add(d, total):
        other = lax.rem(me + n - d, n)
        arrive(other).wait_recv()
        return total + recv[other]

    total = lax.fori_loop(1, n, add, terms[row, col])
    out[col] = total

    def share(to_col):
        return pltpu.make_async_remote_copy(
            src_ref=out.at[col],
            dst_ref=out.at[col],
            send_sem=send2.at[to_col],
            recv_sem=recv2.at[col],
            device_id=(row, to_col),
            device_id_type=MESH,
        )

    def shared(from_col):
        return pltpu.make_async_remote_copy(
            src_ref=out.at[from_col],
            dst_ref=out.at[from_col],
            send_sem=send2.at[from_col],
            recv_sem=recv2.at[from_col],
            device_id=(row, from_col),
            device_id_type=MESH,
        )

    def start2(d, carry):
        share(lax.rem(col + d, n_col)).start()
        return carry

    lax.fori_loop(1, n_col, start2, 0)

    def end1(d, carry):
        spread(lax.rem(me + d, n)).wait_send()
        return carry

    lax.fori_loop(1, n, end1, 0)

    def end2(d, carry):
        shared(lax.rem(col + n_col - d, n_col)).wait_recv()
        share(lax.rem(col + d, n_col)).wait_send()
        return carry

    lax.fori_loop(1, n_col, end2, 0)


def sum_terms(terms, n_row, n_col):
    members, width, _ = terms.shape
    n = n_row * n_col
    lanes = 128
    depth = members * width * width // (n * lanes)
    terms = terms.reshape(members, n_row, width // n_row, width).transpose(1, 0, 2, 3)
    terms = terms.reshape(n_row, n_col, depth, lanes)
    total = pl.pallas_call(
        functools.partial(sum_kernel, n_row, n_col),
        out_shape=jax.ShapeDtypeStruct((n_col, depth, lanes), jnp.float32),
        in_specs=[pl.BlockSpec(memory_space=pltpu.VMEM)],
        out_specs=pl.BlockSpec(memory_space=pltpu.VMEM),
        scratch_shapes=[
            pltpu.VMEM((n, depth, lanes), jnp.float32),
            pltpu.SemaphoreType.DMA((n,)),
            pltpu.SemaphoreType.DMA((n,)),
            pltpu.SemaphoreType.DMA((n_col,)),
            pltpu.SemaphoreType.DMA((n_col,)),
        ],
        compiler_params=pltpu.CompilerParams(collective_id=1, has_side_effects=True),
        name="sum_terms",
    )(terms)
    return total.reshape(members, width // n_row, width)


def product_kernel(n_row, n_col, s_ref, x_ref, out, hop, xc, xs, hi, lo, stage, part_sum, sib, run,
                   load, s0, r0, s1, r1, s2, r2, s3, r3, s4, r4):
    n = n_row * n_col
    chips = n_col // 2
    members, local_rows, _ = x_ref.shape
    splits, part = xc.shape[2], xc.shape[3]
    group = n_row // splits
    row, col = lax.axis_index("row"), lax.axis_index("col")
    me = row * n_col + col
    chip, core = col // 2, lax.rem(col, 2)
    member_i = lax.rem(col, n_row)
    my_split = row // group
    first_i = lax.rem(row, group) * splits
    relay = lax.rem(row, group) == member_i // splits

    barrier = pltpu.get_barrier_semaphore()

    def greet(d, carry):
        other = lax.rem(me + d, n)
        pl.semaphore_signal(
            barrier, inc=1, device_id=(other // n_col, lax.rem(other, n_col)), device_id_type=MESH
        )
        return carry

    lax.fori_loop(1, n, greet, 0)
    pl.semaphore_wait(barrier, n - 1)

    def remote(src, dst, send, recv, to):
        return pltpu.make_async_remote_copy(
            src_ref=src, dst_ref=dst, send_sem=send, recv_sem=recv, device_id=to, device_id_type=MESH
        )

    def hop0(k, q):
        to_row = q * group + member_i // splits
        return to_row, remote(
            x_ref.at[k, pl.ds(q * part, part)], hop.at[k, row], s0.at[k, q], r0.at[k, row], (to_row, col)
        )

    def hop1(k, from_row):
        to_col = (from_row * n_col + col) // n_row
        return to_col, remote(
            hop.at[k, from_row],
            xc.at[k, member_i, my_split],
            s1.at[k, from_row],
            r1.at[k, lax.rem(member_i, splits)],
            (row, to_col),
        )

    def hop2(k, d):
        to_row = lax.rem(row + d, n_row)
        block = xc.at[k, pl.ds(first_i, splits), my_split]
        return remote(block, block, s2.at[k, to_row], r2.at[k, row], (to_row, col))

    for k in range(members):
        for q in range(splits):
            to_row, copy = hop0(k, q)
            pl.when(to_row != row)(copy.start)

    chunk = stage.shape[1]
    chunks = s_ref.shape[0] // chunk

    def fetch(i):
        slot = lax.rem(i, 2)
        return pltpu.make_async_copy(
            s_ref.at[pl.ds(i * chunk, chunk)], stage.at[slot], load.at[slot]
        )

    fetch(0).start()

    def split_rows(i, carry):
        @pl.when(i + 1 < chunks)
        def _():
            fetch(i + 1).start()

        fetch(i).wait()
        value = stage[lax.rem(i, 2)]
        upper = value.astype(jnp.bfloat16)
        rows = pl.ds(pl.multiple_of(i * chunk, chunk), chunk)
        hi[rows, :] = upper
        lo[rows, :] = (value - upper.astype(jnp.float32)).astype(jnp.bfloat16)
        return carry

    third = chunks // 3
    lax.fori_loop(0, third, split_rows, 0)

    for k in range(members):

        @pl.when(relay)
        def _():
            hop[k, row] = x_ref[k, pl.ds(pl.multiple_of(my_split * part, 8), part), :]
            for d in range(1, n_row):
                from_row = lax.rem(row + d, n_row)
                remote(
                    hop.at[k, from_row], hop.at[k, from_row], s0.at[k, 0], r0.at[k, from_row], (row, col)
                ).wait_recv()
            for from_row in range(n_row):
                to_col, copy = hop1(k, from_row)
                pl.when(to_col != col)(copy.start)

                @pl.when(to_col == col)
                def _():
                    xc[k, member_i, my_split] = hop[k, from_row]

    lax.fori_loop(third, 2 * third, split_rows, 0)

    for k in range(members):
        for s in range(splits):
            from_col = lax.rem(col * n_row + first_i + s, n_col)
            block = xc.at[k, first_i + s, my_split]

            @pl.when(from_col != col)
            def _():
                remote(block, block, s1.at[k, 0], r1.at[k, s], (row, col)).wait_recv()

        for d in range(1, n_row):
            hop2(k, d).start()

    lax.fori_loop(2 * third, chunks, split_rows, 0)

    def sibling(k, t):
        return remote(
            part_sum.at[k, 2 * t + 1 - core], sib.at[k, t], s3.at[k, t], r3.at[k, t],
            (row, 2 * chip + 1 - core),
        )

    width = x_ref.shape[2]

    def multiply(k):
        for d in range(1, n_row):
            from_row = lax.rem(row + d, n_row)
            block = xc.at[k, pl.ds(lax.rem(from_row, group) * splits, splits), from_row // group]
            remote(block, block, s2.at[k, 0], r2.at[k, from_row], (row, col)).wait_recv()
        for i in range(n_row):
            value = xc[k, i].reshape(local_rows, width)
            upper = value.astype(jnp.bfloat16)
            rows = pl.ds(i * local_rows, local_rows)
            xs[rows, :width] = upper
            xs[rows, width:] = (value - upper.astype(jnp.float32)).astype(jnp.bfloat16)

        def owner_rows(j, carry):
            t = lax.rem(j, chips)
            owner = 2 * t + lax.rem(core + 1 + j // chips, 2)
            rows = pl.ds(pl.multiple_of(owner * local_rows, 16), local_rows)
            both = jnp.dot(hi[rows, :], xs[...], preferred_element_type=jnp.float32)
            rest = jnp.dot(lo[rows, :], xs[:, :width], preferred_element_type=jnp.float32)
            part_sum[k, owner] = both[:, :width] + (both[:, width:] + rest)

            @pl.when(j < chips)
            def _():
                sibling(k, t).start()

            return carry

        lax.fori_loop(0, n_col, owner_rows, 0)

    def passed(k, t, slot, to_chip):
        return remote(
            part_sum.at[k, 2 * t + core], run.at[k, slot], s4.at[k, t], r4.at[k, slot],
            (row, 2 * to_chip + core),
        )

    def arrived(k, slot):
        return remote(
            run.at[k, slot], run.at[k, slot], s4.at[k, 0], r4.at[k, slot], (row, col)
        )

    def begin(k):
        for t in range(chips):
            sibling(k, t).wait()
            part_sum[k, 2 * t + core] += sib[k, t]

        @pl.when(chip == 0)
        def _():
            for t in range(chips - 1, 0, -1):
                passed(k, t, t + 1, chip + 1).start()

        @pl.when(chip == chips - 1)
        def _():
            for t in range(chips - 1):
                passed(k, t, t, chip - 1).start()

    def forward(k):
        for j in range(chips - 1):
            t = chips - 1 - j

            @pl.when((chip < t) & (chip > 0))
            def _():
                arrived(k, t + 1).wait_recv()
                part_sum[k, 2 * t + core] += run[k, t + 1]
                passed(k, t, t + 1, chip + 1).start()

            @pl.when((chip > j) & (chip < chips - 1))
            def _():
                arrived(k, j).wait_recv()
                part_sum[k, 2 * j + core] += run[k, j]
                passed(k, j, j, chip - 1).start()

    def finish(k):
        out[k] = part_sum[k, col]

        @pl.when(chip > 0)
        def _():
            arrived(k, chip + 1).wait_recv()
            out[k] += run[k, chip + 1]

        @pl.when(chip < chips - 1)
        def _():
            arrived(k, chip).wait_recv()
            out[k] += run[k, chip]

    for k in range(members):
        multiply(k)
        begin(k)
        if k > 0:
            forward(k - 1)
    forward(members - 1)
    for k in range(members):
        finish(k)

    for k in range(members):
        for q in range(splits):
            to_row, copy = hop0(k, q)
            pl.when(to_row != row)(copy.wait_send)

        @pl.when(relay)
        def _():
            for from_row in range(n_row):
                to_col, copy = hop1(k, from_row)
                pl.when(to_col != col)(copy.wait_send)

        for d in range(1, n_row):
            hop2(k, d).wait_send()
        for t in range(chips):

            @pl.when(chip < t)
            def _():
                passed(k, t, t + 1, chip + 1).wait_send()

            @pl.when(chip > t)
            def _():
                passed(k, t, t, chip - 1).wait_send()


def product(inverse_block, masked_local, n_row, n_col):
    members, local_rows, width = masked_local.shape
    span_row, span_col = inverse_block.shape
    chips = n_col // 2
    splits = max(d for d in range(1, n_row + 1) if n_row % d == 0 and local_rows % (8 * d) == 0)
    part = local_rows // splits
    chunk = span_row // 24
    f32, bf16, sem = jnp.float32, jnp.bfloat16, pltpu.SemaphoreType.DMA
    scratch = [
        ((members, n_row, part, width), f32),
        ((members, n_row, splits, part, width), f32),
        ((span_col, 2 * width), bf16),
        ((span_row, span_col), bf16),
        ((span_row, span_col), bf16),
        ((2, chunk, span_col), f32),
        ((members, n_col, local_rows, width), f32),
        ((members, chips, local_rows, width), f32),
        ((members, chips + 1, local_rows, width), f32),
    ]
    macs = members * span_row * span_col * width
    return pl.pallas_call(
        functools.partial(product_kernel, n_row, n_col),
        out_shape=jax.ShapeDtypeStruct(masked_local.shape, f32),
        in_specs=[pl.BlockSpec(memory_space=pl.ANY), pl.BlockSpec(memory_space=pltpu.VMEM)],
        out_specs=pl.BlockSpec(memory_space=pltpu.VMEM),
        scratch_shapes=[pltpu.VMEM(shape, kind) for shape, kind in scratch]
        + [
            sem((2,)),
            sem((members, splits)), sem((members, n_row)),
            sem((members, n_row)), sem((members, splits)),
            sem((members, n_row)), sem((members, n_row)),
            sem((members, chips)), sem((members, chips)),
            sem((members, chips)), sem((members, chips + 1)),
        ],
        compiler_params=pltpu.CompilerParams(
            collective_id=2, has_side_effects=True, vmem_limit_bytes=60 * 2**20
        ),
        cost_estimate=pl.CostEstimate(
            flops=6 * macs, bytes_accessed=4 * span_row * span_col, transcendentals=0
        ),
        name="product",
    )(inverse_block, masked_local)


def per_device(n_row, n_col, inverse_block, factor_panel, diag_inverse, block_lists, list_counts):
    row_id = lax.axis_index("row")
    col_id = lax.axis_index("col")
    members, local_rows, _ = factor_panel.shape
    nblocks = block_lists.shape[1]
    block = local_rows * n_row * n_col // nblocks
    n = n_row * n_col
    table = listed_table(block_lists, list_counts, nblocks)
    mask_local = rows_mask(table, (row_id * n_col + col_id) * local_rows, local_rows, block)
    masked_local = jnp.where(mask_local[:, :, None], factor_panel, 0.0)
    solved = jnp.where(mask_local[:, :, None], -product(inverse_block, masked_local, n_row, n_col), 0.0)
    terms = jnp.einsum("knw,knv->kwv", masked_local, solved, precision=lax.Precision.HIGHEST)
    return (solved, diag_inverse - sum_terms(terms, n_row, n_col))


def solution(mesh):
    n_row, n_col = mesh.shape["row"], mesh.shape["col"]
    placed = (P("row", "col"), P(None, ("row", "col"), None), P(None, "row", None), P(), P())
    return jax.shard_map(
        functools.partial(per_device, n_row, n_col),
        mesh=mesh,
        in_specs=placed,
        out_specs=(P(None, ("row", "col"), None), P(None, "row", None)),
        check_vma=False,
    )
```

```python
import functools

import jax
import jax.numpy as jnp
from jax import lax
from jax.experimental import pallas as pl
from jax.experimental.pallas import tpu as pltpu
from jax.sharding import PartitionSpec as P

MESH = pl.DeviceIdType.MESH


def listed_table(block_lists, list_counts, nblocks):
    entries = jnp.arange(block_lists.shape[1], dtype=jnp.int32)
    active = entries[None, :] < list_counts[:, None]
    hits = (
        block_lists[:, :, None] == jnp.arange(nblocks, dtype=jnp.int32)[None, None, :]
    ) & active[:, :, None]
    return jnp.any(hits, axis=1).astype(jnp.float32)


def rows_mask(table, first_row, count, block):
    global_rows = first_row + jnp.arange(count, dtype=jnp.int32)
    onehot = (global_rows // block)[:, None] == jnp.arange(table.shape[1], dtype=jnp.int32)[None, :]
    return jnp.any(onehot[None] & (table > 0)[:, None, :], axis=2)


def sum_kernel(n_row, n_col, terms, out, swap, half, by_row, line, by_chip, s0, r0, s1, r1, s2, r2, s3, r3):
    chips = n_col // 2
    row, col = lax.axis_index("row"), lax.axis_index("col")
    chip, core = col // 2, lax.rem(col, 2)
    barrier = pltpu.get_barrier_semaphore()
    for d in range(1, n_row):
        pl.semaphore_signal(
            barrier, inc=1, device_id=(lax.rem(row + d, n_row), col), device_id_type=MESH
        )
    for d in range(1, n_col):
        pl.semaphore_signal(
            barrier, inc=1, device_id=(row, lax.rem(col + d, n_col)), device_id_type=MESH
        )
    pl.semaphore_wait(barrier, n_row + n_col - 2)

    def remote(src, dst, send, recv, to):
        return pltpu.make_async_remote_copy(
            src_ref=src, dst_ref=dst, send_sem=send, recv_sem=recv, device_id=to, device_id_type=MESH
        )

    pair = remote(terms.at[1 - core], swap, s0.at[0], r0.at[0], (row, 2 * chip + 1 - core))
    pair.start()
    pair.wait()
    half[...] = terms[core] + swap[...]

    def to_row(d):
        other = lax.rem(row + d, n_row)
        return remote(half.at[other], by_row.at[row], s1.at[other], r1.at[row], (other, col))

    def to_chip(d):
        other = lax.rem(chip + d, chips)
        return remote(
            line.at[other], by_chip.at[chip], s2.at[other], r2.at[chip], (row, 2 * other + core)
        )

    def to_col(d):
        other = lax.rem(col + d, n_col)
        return remote(out.at[col], out.at[col], s3.at[other], r3.at[col], (row, other))

    for d in range(1, n_row):
        to_row(d).start()
    line[...] = half[row]
    for d in range(1, n_row):
        other = lax.rem(row + n_row - d, n_row)
        slot = by_row.at[other]
        remote(slot, slot, s1.at[other], r1.at[other], (row, col)).wait_recv()
        line[...] += by_row[other]
    for d in range(1, chips):
        to_chip(d).start()
    total = line[chip]
    for d in range(1, chips):
        other = lax.rem(chip + chips - d, chips)
        slot = by_chip.at[other]
        remote(slot, slot, s2.at[other], r2.at[other], (row, col)).wait_recv()
        total += by_chip[other]
    out[col] = total
    for d in range(1, n_col):
        to_col(d).start()
    for d in range(1, n_col):
        other = lax.rem(col + n_col - d, n_col)
        slot = out.at[other]
        remote(slot, slot, s3.at[other], r3.at[other], (row, col)).wait_recv()
    for d in range(1, n_row):
        to_row(d).wait_send()
    for d in range(1, chips):
        to_chip(d).wait_send()
    for d in range(1, n_col):
        to_col(d).wait_send()


def sum_terms(terms, n_row, n_col):
    members, width, _ = terms.shape
    chips, lanes = n_col // 2, 128
    depth = members * width * width // (n_row * n_col * lanes)
    terms = terms.reshape(members, n_row, width // n_row, width).transpose(1, 0, 2, 3)
    terms = terms.reshape(n_row, chips, 2, depth, lanes).transpose(2, 0, 1, 3, 4)
    f32, sem = jnp.float32, pltpu.SemaphoreType.DMA
    total = pl.pallas_call(
        functools.partial(sum_kernel, n_row, n_col),
        out_shape=jax.ShapeDtypeStruct((n_col, depth, lanes), f32),
        in_specs=[pl.BlockSpec(memory_space=pltpu.VMEM)],
        out_specs=pl.BlockSpec(memory_space=pltpu.VMEM),
        scratch_shapes=[
            pltpu.VMEM((n_row, chips, depth, lanes), f32),
            pltpu.VMEM((n_row, chips, depth, lanes), f32),
            pltpu.VMEM((n_row, chips, depth, lanes), f32),
            pltpu.VMEM((chips, depth, lanes), f32),
            pltpu.VMEM((chips, depth, lanes), f32),
            sem((1,)), sem((1,)),
            sem((n_row,)), sem((n_row,)),
            sem((chips,)), sem((chips,)),
            sem((n_col,)), sem((n_col,)),
        ],
        compiler_params=pltpu.CompilerParams(collective_id=1, has_side_effects=True),
        name="sum_terms",
    )(terms)
    return total.reshape(members, width // n_row, width)


def product_kernel(n_row, n_col, s_ref, x_ref, out, hop, xc, xs, hi, lo, stage, part_sum, sib, run,
                   load, s0, r0, s1, r1, s2, r2, s3, r3, s4, r4):
    n = n_row * n_col
    chips = n_col // 2
    members, local_rows, _ = x_ref.shape
    splits, part = xc.shape[2], xc.shape[3]
    group = n_row // splits
    row, col = lax.axis_index("row"), lax.axis_index("col")
    me = row * n_col + col
    chip, core = col // 2, lax.rem(col, 2)
    member_i = lax.rem(col, n_row)
    my_split = row // group
    first_i = lax.rem(row, group) * splits
    relay = lax.rem(row, group) == member_i // splits

    barrier = pltpu.get_barrier_semaphore()

    def greet(d, carry):
        other = lax.rem(me + d, n)
        pl.semaphore_signal(
            barrier, inc=1, device_id=(other // n_col, lax.rem(other, n_col)), device_id_type=MESH
        )
        return carry

    lax.fori_loop(1, n, greet, 0)
    pl.semaphore_wait(barrier, n - 1)

    def remote(src, dst, send, recv, to):
        return pltpu.make_async_remote_copy(
            src_ref=src, dst_ref=dst, send_sem=send, recv_sem=recv, device_id=to, device_id_type=MESH
        )

    def hop0(k, q):
        to_row = q * group + member_i // splits
        return to_row, remote(
            x_ref.at[k, pl.ds(q * part, part)], hop.at[k, row], s0.at[k, q], r0.at[k, row], (to_row, col)
        )

    def hop1(k, from_row):
        to_col = (from_row * n_col + col) // n_row
        return to_col, remote(
            hop.at[k, from_row],
            xc.at[k, member_i, my_split],
            s1.at[k, from_row],
            r1.at[k, lax.rem(member_i, splits)],
            (row, to_col),
        )

    def hop2(k, d):
        to_row = lax.rem(row + d, n_row)
        block = xc.at[k, pl.ds(first_i, splits), my_split]
        return remote(block, block, s2.at[k, to_row], r2.at[k, row], (to_row, col))

    for k in range(members):
        for q in range(splits):
            to_row, copy = hop0(k, q)
            pl.when(to_row != row)(copy.start)

    chunk = stage.shape[1]
    chunks = s_ref.shape[0] // chunk

    def fetch(i):
        slot = lax.rem(i, 2)
        return pltpu.make_async_copy(
            s_ref.at[pl.ds(i * chunk, chunk)], stage.at[slot], load.at[slot]
        )

    fetch(0).start()

    def split_rows(i, carry):
        @pl.when(i + 1 < chunks)
        def _():
            fetch(i + 1).start()

        fetch(i).wait()
        value = stage[lax.rem(i, 2)]
        upper = value.astype(jnp.bfloat16)
        rows = pl.ds(pl.multiple_of(i * chunk, chunk), chunk)
        hi[rows, :] = upper
        lo[rows, :] = (value - upper.astype(jnp.float32)).astype(jnp.bfloat16)
        return carry

    third = chunks // 3
    lax.fori_loop(0, third, split_rows, 0)

    for k in range(members):

        @pl.when(relay)
        def _():
            hop[k, row] = x_ref[k, pl.ds(pl.multiple_of(my_split * part, 8), part), :]
            for d in range(1, n_row):
                from_row = lax.rem(row + d, n_row)
                remote(
                    hop.at[k, from_row], hop.at[k, from_row], s0.at[k, 0], r0.at[k, from_row], (row, col)
                ).wait_recv()
            for from_row in range(n_row):
                to_col, copy = hop1(k, from_row)
                pl.when(to_col != col)(copy.start)

                @pl.when(to_col == col)
                def _():
                    xc[k, member_i, my_split] = hop[k, from_row]

    lax.fori_loop(third, 2 * third, split_rows, 0)

    for k in range(members):
        for s in range(splits):
            from_col = lax.rem(col * n_row + first_i + s, n_col)
            block = xc.at[k, first_i + s, my_split]

            @pl.when(from_col != col)
            def _():
                remote(block, block, s1.at[k, 0], r1.at[k, s], (row, col)).wait_recv()

        for d in range(1, n_row):
            hop2(k, d).start()

    lax.fori_loop(2 * third, chunks, split_rows, 0)

    def sibling(k, t):
        return remote(
            part_sum.at[k, 2 * t + 1 - core], sib.at[k, t], s3.at[k, t], r3.at[k, t],
            (row, 2 * chip + 1 - core),
        )

    width = x_ref.shape[2]

    def multiply(k):
        for d in range(1, n_row):
            from_row = lax.rem(row + d, n_row)
            block = xc.at[k, pl.ds(lax.rem(from_row, group) * splits, splits), from_row // group]
            remote(block, block, s2.at[k, 0], r2.at[k, from_row], (row, col)).wait_recv()
        for i in range(n_row):
            value = xc[k, i].reshape(local_rows, width)
            upper = value.astype(jnp.bfloat16)
            rows = pl.ds(i * local_rows, local_rows)
            xs[rows, :width] = upper
            xs[rows, width:] = (value - upper.astype(jnp.float32)).astype(jnp.bfloat16)

        def owner_rows(j, carry):
            t = lax.rem(j, chips)
            owner = 2 * t + lax.rem(core + 1 + j // chips, 2)
            rows = pl.ds(pl.multiple_of(owner * local_rows, 16), local_rows)
            both = jnp.dot(hi[rows, :], xs[...], preferred_element_type=jnp.float32)
            rest = jnp.dot(lo[rows, :], xs[:, :width], preferred_element_type=jnp.float32)
            part_sum[k, owner] = both[:, :width] + (both[:, width:] + rest)

            @pl.when(j < chips)
            def _():
                sibling(k, t).start()

            return carry

        lax.fori_loop(0, n_col, owner_rows, 0)

    def passed(k, t, slot, to_chip):
        return remote(
            part_sum.at[k, 2 * t + core], run.at[k, slot], s4.at[k, t], r4.at[k, slot],
            (row, 2 * to_chip + core),
        )

    def arrived(k, slot):
        return remote(
            run.at[k, slot], run.at[k, slot], s4.at[k, 0], r4.at[k, slot], (row, col)
        )

    def begin(k):
        for t in range(chips):
            sibling(k, t).wait()
            part_sum[k, 2 * t + core] += sib[k, t]

        @pl.when(chip == 0)
        def _():
            for t in range(chips - 1, 0, -1):
                passed(k, t, t + 1, chip + 1).start()

        @pl.when(chip == chips - 1)
        def _():
            for t in range(chips - 1):
                passed(k, t, t, chip - 1).start()

    def forward(k):
        for j in range(chips - 1):
            t = chips - 1 - j

            @pl.when((chip < t) & (chip > 0))
            def _():
                arrived(k, t + 1).wait_recv()
                part_sum[k, 2 * t + core] += run[k, t + 1]
                passed(k, t, t + 1, chip + 1).start()

            @pl.when((chip > j) & (chip < chips - 1))
            def _():
                arrived(k, j).wait_recv()
                part_sum[k, 2 * j + core] += run[k, j]
                passed(k, j, j, chip - 1).start()

    def finish(k):
        out[k] = part_sum[k, col]

        @pl.when(chip > 0)
        def _():
            arrived(k, chip + 1).wait_recv()
            out[k] += run[k, chip + 1]

        @pl.when(chip < chips - 1)
        def _():
            arrived(k, chip).wait_recv()
            out[k] += run[k, chip]

    for k in range(members):
        multiply(k)
        begin(k)
        if k > 0:
            forward(k - 1)
    forward(members - 1)
    for k in range(members):
        finish(k)

    for k in range(members):
        for q in range(splits):
            to_row, copy = hop0(k, q)
            pl.when(to_row != row)(copy.wait_send)

        @pl.when(relay)
        def _():
            for from_row in range(n_row):
                to_col, copy = hop1(k, from_row)
                pl.when(to_col != col)(copy.wait_send)

        for d in range(1, n_row):
            hop2(k, d).wait_send()
        for t in range(chips):

            @pl.when(chip < t)
            def _():
                passed(k, t, t + 1, chip + 1).wait_send()

            @pl.when(chip > t)
            def _():
                passed(k, t, t, chip - 1).wait_send()


def product(inverse_block, masked_local, n_row, n_col):
    members, local_rows, width = masked_local.shape
    span_row, span_col = inverse_block.shape
    chips = n_col // 2
    splits = max(d for d in range(1, n_row + 1) if n_row % d == 0 and local_rows % (8 * d) == 0)
    part = local_rows // splits
    chunk = span_row // 24
    f32, bf16, sem = jnp.float32, jnp.bfloat16, pltpu.SemaphoreType.DMA
    scratch = [
        ((members, n_row, part, width), f32),
        ((members, n_row, splits, part, width), f32),
        ((span_col, 2 * width), bf16),
        ((span_row, span_col), bf16),
        ((span_row, span_col), bf16),
        ((2, chunk, span_col), f32),
        ((members, n_col, local_rows, width), f32),
        ((members, chips, local_rows, width), f32),
        ((members, chips + 1, local_rows, width), f32),
    ]
    macs = members * span_row * span_col * width
    return pl.pallas_call(
        functools.partial(product_kernel, n_row, n_col),
        out_shape=jax.ShapeDtypeStruct(masked_local.shape, f32),
        in_specs=[pl.BlockSpec(memory_space=pl.ANY), pl.BlockSpec(memory_space=pltpu.VMEM)],
        out_specs=pl.BlockSpec(memory_space=pltpu.VMEM),
        scratch_shapes=[pltpu.VMEM(shape, kind) for shape, kind in scratch]
        + [
            sem((2,)),
            sem((members, splits)), sem((members, n_row)),
            sem((members, n_row)), sem((members, splits)),
            sem((members, n_row)), sem((members, n_row)),
            sem((members, chips)), sem((members, chips)),
            sem((members, chips)), sem((members, chips + 1)),
        ],
        compiler_params=pltpu.CompilerParams(
            collective_id=2, has_side_effects=True, vmem_limit_bytes=60 * 2**20
        ),
        cost_estimate=pl.CostEstimate(
            flops=6 * macs, bytes_accessed=4 * span_row * span_col, transcendentals=0
        ),
        name="product",
    )(inverse_block, masked_local)


def per_device(n_row, n_col, inverse_block, factor_panel, diag_inverse, block_lists, list_counts):
    row_id = lax.axis_index("row")
    col_id = lax.axis_index("col")
    members, local_rows, _ = factor_panel.shape
    nblocks = block_lists.shape[1]
    block = local_rows * n_row * n_col // nblocks
    n = n_row * n_col
    table = listed_table(block_lists, list_counts, nblocks)
    mask_local = rows_mask(table, (row_id * n_col + col_id) * local_rows, local_rows, block)
    masked_local = jnp.where(mask_local[:, :, None], factor_panel, 0.0)
    solved = jnp.where(mask_local[:, :, None], -product(inverse_block, masked_local, n_row, n_col), 0.0)
    terms = jnp.einsum("knw,knv->kwv", masked_local, solved, precision=lax.Precision.HIGHEST)
    return (solved, diag_inverse - sum_terms(terms, n_row, n_col))


def solution(mesh):
    n_row, n_col = mesh.shape["row"], mesh.shape["col"]
    placed = (P("row", "col"), P(None, ("row", "col"), None), P(None, "row", None), P(), P())
    return jax.shard_map(
        functools.partial(per_device, n_row, n_col),
        mesh=mesh,
        in_specs=placed,
        out_specs=(P(None, ("row", "col"), None), P(None, "row", None)),
        check_vma=False,
    )
```
